32 devices in a mesh: pipe: 4 (over y, x), dp: 2 (over core), expert: 4 (over z).
Axes of the slice: x: 2, y: 2, z: 4, core: 2. Of those that a mesh axis runs over, the one named last changes fastest.
Arguments:
- fwd_tokens: bfloat16 [4, 512, 7168], P('pipe', 'expert'), may hold values from -6 to 6
- fwd_routes: int32 [4, 512, 2], P('pipe', 'expert'), may hold values from 0 to 3, all different within a row; in each aligned block of 128 rows (0 to 127, 128 to 255, ..., all dimensions but the last counted through in order) at most 96 rows name the same one
- fwd_gates: float32 [4, 512, 2], P('pipe', 'expert'), may hold values from 0.2 to 1
- bwd_saved: bfloat16 [4, 512, 7168], P('pipe', 'expert'), may hold values from -6 to 6
- bwd_grads: bfloat16 [4, 512, 7168], P('pipe', 'expert'), may hold values from -6 to 6
- bwd_routes: int32 [4, 512, 2], P('pipe', 'expert'), may hold values from 0 to 3, all different within a row; in each aligned block of 128 rows (0 to 127, 128 to 255, ..., all dimensions but the last counted through in order) at most 96 rows name the same one
- bwd_gates: float32 [4, 512, 2], P('pipe', 'expert'), may hold values from 0.2 to 1
- w_up: bfloat16 [4, 4, 7168, 1024], P('pipe', 'expert', None, 'dp'), may hold values from -0.0625 to 0.0625
- w_down: bfloat16 [4, 4, 1024, 7168], P('pipe', 'expert', 'dp'), may hold values from -0.1875 to 0.1875
- query_latent: bfloat16 [4, 2, 1024, 768], P('pipe', 'dp', 'expert'), may hold values from -6 to 6
- key_latent: bfloat16 [4, 2, 1024, 512], P('pipe', 'dp', 'expert'), may hold values from -6 to 6
- query_weight: bfloat16 [4, 768, 8192], P('pipe', None, 'expert'), may hold values from -500 to 500
- key_weight: bfloat16 [4, 512, 8192], P('pipe', None, 'expert'), may hold values from -0.25 to 0.25
Outputs:
- fwd_arrive: bfloat16 [4, 512, 7168], P('pipe', 'expert')
- bwd_arrive: bfloat16 [4, 512, 7168], P('pipe', 'expert')
- query_clipped: bfloat16 [4, 768, 8192], P('pipe', None, 'expert')
- key_clipped: bfloat16 [4, 512, 8192], P('pipe', None, 'expert')
The draws below stay inside these ranges and needn't reach their ends.
Inputs may be any that keep to these rules, and one draw needn't show every extreme that they name: `fwd_routes`: within the rows of one device (aligned blocks of 128 token rows of a section) no expert is named by more than 96 rows, a bound that some block reaches. `bwd_routes`: within the rows of one device (aligned blocks of 128 token rows of a section) no expert is named by more than 96 rows, a bound that some block reaches.
All inputs are finite; a program needn't handle non-finite values.
Results may differ from the reference program's by a relative error of at most 0.0046.
Values may be sent and summed in bfloat16 or wider, within the bound.
A program may use at most 192 MiB of HBM per device.

```python
import math
import jax
import jax.numpy as jnp
import numpy as np
from jax import lax

D = 7168
HID = 1024
HEADS = 64
HD = 128
QR = 768
KR = 512
TOP = 2
TOK_DEV = 128
SEQ = 1024
EXPERTS = 4
TOKENS = 512
CAP = 96
N_PIPE = 4
N_DP = 2
N_EXPERT = 4


def draw_query_weight(key, part):
    level_random_key = jax.random.fold_in(key, 11)
    value_key = jax.random.fold_in(key, 23)
    level = jax.random.uniform(level_random_key, (N_PIPE, 1, HEADS, 1), jnp.float32, math.log(4.0), math.log(100.0))
    base = jnp.clip(jax.random.normal(value_key, (N_PIPE, QR, HEADS, HD), jnp.float32), -5.0, 5.0)
    values = base * jnp.exp(level) * QR ** (-0.5)
    return values.reshape(N_PIPE, QR, HEADS * HD).astype(jnp.bfloat16)


def levels(key, shape, pieces, least, largest):
    def one(axis_at, shards_of):
        draws = jax.random.uniform(jax.random.fold_in(jax.random.fold_in(key, 6), axis_at), (shards_of,), jnp.float32, least / len(pieces), largest / len(pieces))
        return jnp.repeat(jnp.exp(draws), shape[axis_at] // shards_of).reshape((-1,) + (1,) * (len(shape) - axis_at - 1))

    level = one(*pieces[0])
    for cut in pieces[1:]:
        level = level * one(*cut)
    return level


def routed_block(stream_key, own, number, rows, count, top, reach, slope):
    order = jax.random.permutation(stream_key, count)
    packed, ordinary = portions_of(count, rows * top, reach, slope, True), portions_of(count, rows * top, reach, slope, False)
    places = jnp.arange(count)

    def named(lengths, offset_by):
        used = int((lengths > 0).sum())
        fixed = max(1, used // 4)
        shifted = fixed + (places - fixed + offset_by * (used - fixed)) % max(1, count - fixed)
        return jnp.zeros((count,), jnp.int32).at[order[jnp.where(places < fixed, places, shifted)]].set(jnp.asarray(lengths, jnp.int32))

    lengths = jnp.where(number % 4 == 0, named(packed, number // 4), named(ordinary, number - number // 4 - 1))
    mixed = jax.random.permutation(jax.random.fold_in(own, 3), count)
    donor, sink = mixed[0:count // 2 * 2:2], mixed[1:count // 2 * 2:2]
    margin = jnp.minimum(lengths[donor] - 1, reach - lengths[sink]) // 2
    margin = jnp.where((donor == order[0]) | (sink == order[0]) | (lengths[sink] == 0), 0, jnp.maximum(margin, 0))
    shifted = jax.random.randint(jax.random.fold_in(own, 4), (count // 2,), 0, 1 << 20) % (margin + 1)
    lengths = lengths.at[donor].add(-shifted).at[sink].add(shifted)
    items = jnp.searchsorted(jnp.cumsum(lengths), jnp.arange(rows * top), side="right").astype(jnp.int32)
    listing = items.reshape(top, rows).T
    listing = listing[jax.random.permutation(jax.random.fold_in(own, 1), rows)]
    offset_by = jax.random.randint(jax.random.fold_in(own, 2), (rows, 1), 0, top)
    return jnp.take_along_axis(listing, (jnp.arange(top)[None, :] + offset_by) % top, axis=1)


def portions_of(amount, total, limit, slope, full):
    portions = [(1 << 20) // math.isqrt(standing ** slope) + 1 for standing in range(1, amount + 1)]
    largest = limit if full else min(limit, max(-(-total // amount), total * portions[0] // sum(portions)))
    least = 1 if total - largest >= amount - 1 else 0
    holding, spare = [largest] + [least] * (amount - 1), total - largest - least * (amount - 1)
    while spare > 0:
        free = [i for i in range(1, amount) if holding[i] < largest] or [i for i in range(1, amount) if holding[i] < limit]
        pool, budget = sum([portions[i] for i in free]), spare
        for i in free:
            addition = min(limit - holding[i], max(1, budget * portions[i] // pool), spare)
            holding[i] = holding[i] + addition
            spare = spare - addition
    return np.array(holding)


def gaussian(key, dims, scale, bound, pieces=(), held_as=jnp.bfloat16):
    result = scale * jax.random.normal(key, dims, jnp.float32)
    if pieces:
        result = result * levels(key, dims, pieces, -0.22, 0.18)
    return jnp.clip(result, -bound, bound).astype(held_as)


def setup_inputs(seed: int = 0) -> dict:
    keys = jax.random.split(jax.random.key(seed), 14)
    fwd_tokens = gaussian(keys[0], (N_PIPE, TOKENS, D), 1.0, 6.0, ((0, 4), (1, 4)))
    fwd_routes_keys = jax.random.split(jax.random.fold_in(keys[1], 1), N_PIPE * TOKENS // TOK_DEV)
    fwd_routes_turns = jax.random.permutation(jax.random.fold_in(keys[1], 3), N_PIPE * TOKENS // TOK_DEV)
    fwd_routes = jax.vmap(lambda own, number: routed_block(jax.random.fold_in(keys[1], 2), own, number, TOK_DEV, EXPERTS, TOP, CAP, 2))(fwd_routes_keys, fwd_routes_turns).reshape((N_PIPE, TOKENS, TOP))
    fwd_gates = jnp.clip(0.2 + 0.8 * jax.random.uniform(keys[2], (N_PIPE, TOKENS, TOP), jnp.float32) ** levels(keys[2], (N_PIPE, TOKENS, TOP), ((0, 4), (1, 4)), -0.2, 0.2), 0.2, 1.0)
    bwd_saved = gaussian(keys[3], (N_PIPE, TOKENS, D), 1.0, 6.0, ((0, 4), (1, 4)))
    bwd_grads = gaussian(keys[4], (N_PIPE, TOKENS, D), 1.0, 6.0, ((0, 4), (1, 4)))
    bwd_routes_keys = jax.random.split(jax.random.fold_in(keys[5], 1), N_PIPE * TOKENS // TOK_DEV)
    bwd_routes_turns = jax.random.permutation(jax.random.fold_in(keys[5], 3), N_PIPE * TOKENS // TOK_DEV)
    bwd_routes = jax.vmap(lambda own, number: routed_block(jax.random.fold_in(keys[5], 2), own, number, TOK_DEV, EXPERTS, TOP, CAP, 2))(bwd_routes_keys, bwd_routes_turns).reshape((N_PIPE, TOKENS, TOP))
    bwd_gates = jnp.clip(0.2 + 0.8 * jax.random.uniform(keys[6], (N_PIPE, TOKENS, TOP), jnp.float32) ** levels(keys[6], (N_PIPE, TOKENS, TOP), ((0, 4), (1, 4)), -0.2, 0.2), 0.2, 1.0)
    w_up = gaussian(keys[7], (N_PIPE, EXPERTS, D, HID), D ** -0.5, 0.0625, ((0, 4), (1, 4), (3, 2)))
    w_down = gaussian(keys[8], (N_PIPE, EXPERTS, HID, D), HID ** -0.5, 0.1875, ((0, 4), (1, 4), (2, 2)))
    query_latent = gaussian(keys[9], (N_PIPE, N_DP, SEQ, QR), 1.0, 6.0, ((0, 4), (1, 2), (2, 4)))
    key_latent = gaussian(keys[10], (N_PIPE, N_DP, SEQ, KR), 1.0, 6.0, ((0, 4), (1, 2), (2, 4)))
    query_weight = draw_query_weight(jax.random.fold_in(keys[13], 71), 0)
    key_weight = gaussian(keys[12], (N_PIPE, KR, HEADS * HD), KR ** -0.5, 0.25, ((0, 4), (2, 4)))
    return dict(fwd_tokens=fwd_tokens, fwd_routes=fwd_routes, fwd_gates=fwd_gates, bwd_saved=bwd_saved, bwd_grads=bwd_grads, bwd_routes=bwd_routes, bwd_gates=bwd_gates, w_up=w_up, w_down=w_down, query_latent=query_latent, key_latent=key_latent, query_weight=query_weight, key_weight=key_weight)


clip_limit = 100.0
logit_scale = 192.0 ** (-0.5)

def silu_grad(pre_act):
    sigmoid_val = jax.nn.sigmoid(pre_act)
    return sigmoid_val * (1.0 + pre_act * (1.0 - sigmoid_val))

def expert_table(flat_ids, expert):
    row_count = flat_ids.shape[0]
    hits = (flat_ids == expert).astype(jnp.int32)
    order = jnp.cumsum(hits) - 1
    goal_value = jnp.where(hits > 0, order, N_EXPERT * CAP).astype(jnp.int32)
    slot_table = jnp.full((N_EXPERT * CAP,), row_count, jnp.int32)
    return slot_table.at[goal_value].set(jnp.arange(row_count, dtype=jnp.int32), mode='drop')

def forward_rows(token_rows, up_half, down_half):
    pre_act = jnp.dot(token_rows[:, 0], up_half, preferred_element_type=jnp.float32)
    hidden = jax.nn.silu(pre_act).astype(jnp.bfloat16)
    return jnp.dot(hidden, down_half, preferred_element_type=jnp.float32)

def backward_rows(token_rows, up_half, down_half):
    pre_act = jnp.dot(token_rows[:, 0], up_half, preferred_element_type=jnp.float32)
    back_grad = jnp.dot(token_rows[:, 1], down_half.T, preferred_element_type=jnp.float32)
    pre_grad = (back_grad * silu_grad(pre_act)).astype(jnp.bfloat16)
    return jnp.dot(pre_grad, up_half.T, preferred_element_type=jnp.float32)

def routed_sum(stacked, routes, gate_vals, up_weight, down_weight, expert_fn):
    flat_ids = routes.reshape(-1)
    row_count = flat_ids.shape[0]
    block_width = HID // N_DP

    def single_expert(buffer, expert):
        slot_table = expert_table(flat_ids, expert)
        source = jnp.minimum(slot_table, row_count - 1) // TOP
        token_rows = stacked[source]
        up_expert = lax.dynamic_index_in_dim(up_weight, expert, 0, keepdims=False)
        down_expert = lax.dynamic_index_in_dim(down_weight, expert, 0, keepdims=False)
        accum = jnp.zeros((token_rows.shape[0], D), jnp.float32)
        for half_idx in range(N_DP):
            up_half = up_expert[:, half_idx * block_width:(half_idx + 1) * block_width]
            down_half = down_expert[half_idx * block_width:(half_idx + 1) * block_width]
            piece_out = expert_fn(token_rows, up_half, down_half).astype(jnp.bfloat16)
            accum = accum + piece_out.astype(jnp.float32)
        buffer = buffer.at[slot_table].set(accum.astype(jnp.bfloat16), mode='drop')
        return (buffer, None)
    buffer = jnp.zeros((row_count, D), jnp.bfloat16)
    buffer, unused = lax.scan(single_expert, buffer, jnp.arange(EXPERTS, dtype=jnp.int32))
    routed = buffer.reshape(routes.shape[0], TOP, D).astype(jnp.float32)
    return lax.optimization_barrier(jnp.sum(gate_vals[:, :, None] * routed, axis=1))

def head_maxima(q_latent, k_latent, query_proj, key_proj):
    queries = jnp.dot(q_latent.reshape(N_DP * SEQ, QR), query_proj, preferred_element_type=jnp.float32)
    queries = queries.astype(jnp.bfloat16).reshape(N_DP, SEQ, HEADS, HD)
    key_rows = jnp.dot(k_latent.reshape(N_DP * SEQ, KR), key_proj, preferred_element_type=jnp.float32)
    key_rows = key_rows.astype(jnp.bfloat16).reshape(N_DP, SEQ, HEADS, HD)
    positions = jnp.arange(SEQ, dtype=jnp.int32)
    allowed = positions[:, None] >= positions[None, :]

    def one_head(head):
        query_head_rows = lax.dynamic_index_in_dim(queries, head, 2, keepdims=False).astype(jnp.float32)
        key_head_rows = lax.dynamic_index_in_dim(key_rows, head, 2, keepdims=False).astype(jnp.float32)
        score_matrix = jnp.einsum('uay,uiy->uai', query_head_rows, key_head_rows) * logit_scale
        score_matrix = jnp.where(allowed[None], score_matrix, -1e+30)
        return jnp.max(score_matrix)
    return lax.map(one_head, jnp.arange(HEADS, dtype=jnp.int32))

def section_work(operands):
    tokens_now, routes_now, gates_now, saved_now, grads_now, broutes_now, bgates_now, up_weight, down_weight, q_latent, k_latent, query_proj, key_proj = operands
    fwd_sum = routed_sum(tokens_now[:, None, :], routes_now, gates_now, up_weight, down_weight, forward_rows)
    section_out = (tokens_now.astype(jnp.float32) + fwd_sum).astype(jnp.bfloat16)
    stacked_back = jnp.stack([saved_now, grads_now], axis=1)
    bwd_sum = routed_sum(stacked_back, broutes_now, bgates_now, up_weight, down_weight, backward_rows)
    input_grad = (grads_now.astype(jnp.float32) + bwd_sum).astype(jnp.bfloat16)
    head_max = head_maxima(q_latent, k_latent, query_proj, key_proj)
    factor = jnp.sqrt(clip_limit / jnp.maximum(head_max, clip_limit))
    col_factor = jnp.repeat(factor, HD)
    query_new = (query_proj.astype(jnp.float32) * col_factor[None, :]).astype(jnp.bfloat16)
    key_new = (key_proj.astype(jnp.float32) * col_factor[None, :]).astype(jnp.bfloat16)
    return (section_out, input_grad, query_new, key_new)

def reference(fwd_tokens, fwd_routes, fwd_gates, bwd_saved, bwd_grads, bwd_routes, bwd_gates, w_up, w_down, query_latent, key_latent, query_weight, key_weight):
    section_out, input_grad, query_new, key_new = lax.map(section_work, (fwd_tokens, fwd_routes, fwd_gates, bwd_saved, bwd_grads, bwd_routes, bwd_gates, w_up, w_down, query_latent, key_latent, query_weight, key_weight))
    fwd_arrive = jnp.concatenate([jnp.zeros_like(section_out[:1]), section_out[:-1]], axis=0)
    bwd_arrive = jnp.concatenate([input_grad[1:], jnp.zeros_like(input_grad[:1])], axis=0)
    return (fwd_arrive, bwd_arrive, query_new, key_new)
```

```python
import jax
import jax.numpy as jnp
from jax import lax
from jax.sharding import PartitionSpec as P

HD = 128

clip_limit = 100.0
logit_scale = 192.0 ** (-0.5)


def silu_grad(pre_act):
    sigmoid_val = jax.nn.sigmoid(pre_act)
    return sigmoid_val * (1.0 + pre_act * (1.0 - sigmoid_val))


def swap(block):
    return lax.ppermute(block, "dp", [(0, 1), (1, 0)])


def own_half(array, axis, core):
    width = array.shape[axis] // 2
    return lax.dynamic_slice_in_dim(array, core * width, width, axis)


def other_half(array, axis, core):
    width = array.shape[axis] // 2
    return lax.dynamic_slice_in_dim(array, (1 - core) * width, width, axis)


def after(block, *earlier):
    return lax.optimization_barrier((block,) + earlier)[0]


def shifted(block, axis, distance):
    devices = range(lax.axis_size(axis))
    route = [(i - distance, i) for i in devices if i - distance in devices]
    return lax.ppermute(block, axis, route)


def spread(block, place):
    n = lax.axis_size("expert")
    up, down = [block], [block]
    for step in range(1, n):
        up.append(lax.ppermute(up[-1], "expert", [(j, j + 1) for j in range(step - 1, n - 1)]))
        down.append(lax.ppermute(down[-1], "expert", [(j, j - 1) for j in range(1, n - step + 1)]))
    blocks = [block] + [jnp.where(place >= r, up[r], down[n - r]) for r in range(1, n)]
    return blocks, (up[min(2, n - 1)], down[min(2, n - 1)])


def collect(parts):
    n = lax.axis_size("expert")
    up = down = None
    for step in range(1, n):
        first, second = parts[step], parts[n - step]
        if up is not None:
            first, second = first + up, second + down
        up = lax.ppermute(first.astype(jnp.bfloat16), "expert", [(j, j + 1) for j in range(0, min(step, n - 1))])
        down = lax.ppermute(
            second.astype(jnp.bfloat16), "expert", [(j, j - 1) for j in range(max(n - step, 1), n)]
        )
        up, down = up.astype(jnp.float32), down.astype(jnp.float32)
    return parts[0] + up + down


def coefficients(routes, gates, place):
    n = lax.axis_size("expert")
    result = []
    for r in range(n):
        target = lax.rem(place + r, n)
        value = jnp.sum(jnp.where(routes == target, gates, 0.0), axis=-1)
        if r:
            value = lax.ppermute(value, "expert", [(j, (j + r) % n) for j in range(n)])
        result.append(value)
    return result


def times(rows, weight):
    return jnp.dot(rows, weight, preferred_element_type=jnp.float32)


def times_transposed(rows, weight):
    return lax.dot_general(rows, weight, (((1,), (1,)), ((), ())), preferred_element_type=jnp.float32)


def on_device(
    fwd_tokens,
    fwd_routes,
    fwd_gates,
    bwd_saved,
    bwd_grads,
    bwd_routes,
    bwd_gates,
    w_up,
    w_down,
    query_latent,
    key_latent,
    query_weight,
    key_weight,
):
    n = lax.axis_size("expert")
    place = lax.axis_index("expert")
    core = lax.axis_index("dp")
    tok = fwd_tokens.shape[1]

    tokens_half = own_half(fwd_tokens[0], 1, core)
    saved_half = own_half(bwd_saved[0], 1, core)
    grads_half = own_half(bwd_grads[0], 1, core)
    routes = jnp.stack([fwd_routes[0], bwd_routes[0]])
    gates = jnp.stack([fwd_gates[0], bwd_gates[0]])
    latent = jnp.concatenate([query_latent[0, 0], key_latent[0, 0]], axis=1)

    tokens_all, mark = spread(tokens_half, place)
    up_own = own_half(w_up[0, 0], 0, core)
    up_other = swap(other_half(w_up[0, 0], 0, core))
    down_own = own_half(w_down[0, 0], 1, core)
    down_other = swap(other_half(w_down[0, 0], 1, core))
    coef = coefficients(routes, gates, place)
    saved_all, mark = spread(after(saved_half, *mark), place)
    grads_all, mark = spread(after(grads_half, *mark), place)
    latent_all, mark = spread(after(latent, *mark), place)

    rows = jnp.concatenate(tokens_all, axis=0)
    pre_act = times(rows, up_own) + swap(times(rows, up_other))
    hidden = jax.nn.silu(pre_act).astype(jnp.bfloat16)
    out = times(hidden, down_own) + times(swap(hidden), down_other)
    parts = [out[r * tok:(r + 1) * tok] * coef[r][0][:, None] for r in range(n)]
    section_half = (tokens_half.astype(jnp.float32) + collect(parts)).astype(jnp.bfloat16)
    fwd_half = shifted(section_half, "pipe", 1)

    rows = jnp.concatenate(saved_all, axis=0)
    pre_act = times(rows, up_own) + swap(times(rows, up_other))
    rows = jnp.concatenate(grads_all, axis=0)
    back = times_transposed(rows, down_own) + swap(times_transposed(rows, down_other))
    pre_grad = (back * silu_grad(pre_act)).astype(jnp.bfloat16)
    out = times_transposed(pre_grad, up_own) + times_transposed(swap(pre_grad), up_other)
    parts = [out[r * tok:(r + 1) * tok] * coef[r][1][:, None] for r in range(n)]
    grad_half = (grads_half.astype(jnp.float32) + collect(parts)).astype(jnp.bfloat16)
    bwd_half = shifted(grad_half, "pipe", -1)

    query_proj = query_weight[0]
    key_proj = key_weight[0]
    heads_here = query_proj.shape[1] // HD
    latents = jnp.concatenate(latent_all, axis=0)
    seq_len = latents.shape[0]
    per = seq_len // n
    owners = lax.rem(place - jnp.arange(n, dtype=jnp.int32) + n, n)
    pos = (owners[:, None] * per + jnp.arange(per, dtype=jnp.int32)[None, :]).reshape(-1)
    rank = query_proj.shape[0]
    queries = times(latents[:, :rank], query_proj).astype(jnp.bfloat16).reshape(seq_len, heads_here, HD)
    keys = times(latents[:, rank:], key_proj).astype(jnp.bfloat16).reshape(seq_len, heads_here, HD)
    scores = jnp.einsum("qhd,khd->hqk", queries, keys, preferred_element_type=jnp.float32) * logit_scale
    scores = jnp.where((pos[:, None] >= pos[None, :])[None], scores, -1e30)
    local_max = jnp.max(scores, axis=(1, 2))
    head_max = jnp.maximum(local_max, swap(local_max))
    factor = jnp.sqrt(clip_limit / jnp.maximum(head_max, clip_limit))
    col_factor = jnp.repeat(factor, HD)
    query_clipped = (query_proj.astype(jnp.float32) * col_factor[None, :]).astype(jnp.bfloat16)
    key_clipped = (key_proj.astype(jnp.float32) * col_factor[None, :]).astype(jnp.bfloat16)

    def whole(half):
        theirs = swap(half)
        first = jnp.where(core == 0, half, theirs)
        second = jnp.where(core == 0, theirs, half)
        return jnp.concatenate([first, second], axis=1)

    return (whole(fwd_half)[None], whole(bwd_half)[None], query_clipped[None], key_clipped[None])


def solution(mesh):
    rows3 = P("pipe", "expert", None)
    in_specs = (rows3,) * 7 + (
        P("pipe", "expert", None, "dp"),
        P("pipe", "expert", "dp", None),
        P("pipe", "dp", "expert", None),
        P("pipe", "dp", "expert", None),
        P("pipe", None, "expert"),
        P("pipe", None, "expert"),
    )
    out_specs = (rows3, rows3, P("pipe", None, "expert"), P("pipe", None, "expert"))
    return jax.shard_map(
        on_device, mesh=mesh, in_specs=in_specs, out_specs=out_specs, check_vma=False
    )
```

```python
import jax
import jax.numpy as jnp
from jax import lax
from jax.sharding import PartitionSpec as P

HD = 128
PIECES = 2

clip_limit = 100.0
logit_scale = 192.0 ** (-0.5)


def silu_grad(pre_act):
    sigmoid_val = jax.nn.sigmoid(pre_act)
    return sigmoid_val * (1.0 + pre_act * (1.0 - sigmoid_val))


def swap(block):
    return lax.ppermute(block, "dp", [(0, 1), (1, 0)])


def own_half(array, axis, core):
    width = array.shape[axis] // 2
    return lax.dynamic_slice_in_dim(array, core * width, width, axis)


def other_half(array, axis, core):
    width = array.shape[axis] // 2
    return lax.dynamic_slice_in_dim(array, (1 - core) * width, width, axis)


def after(block, *earlier):
    return lax.optimization_barrier((block,) + earlier)[0]


def shifted(block, axis, distance):
    devices = range(lax.axis_size(axis))
    route = [(i - distance, i) for i in devices if i - distance in devices]
    return lax.ppermute(block, axis, route)


def spread(block, place):
    n = lax.axis_size("expert")
    up, down = [block], [block]
    for step in range(1, n):
        up.append(lax.ppermute(up[-1], "expert", [(j, j + 1) for j in range(step - 1, n - 1)]))
        down.append(lax.ppermute(down[-1], "expert", [(j, j - 1) for j in range(1, n - step + 1)]))
    blocks = [block] + [jnp.where(place >= r, up[r], down[n - r]) for r in range(1, n)]
    return blocks, (up[min(2, n - 1)], down[min(2, n - 1)]), (up[-1], down[-1])


def collect(parts, behind=()):
    n = lax.axis_size("expert")
    up = down = None
    for step in range(1, n):
        first, second = parts[step], parts[n - step]
        if up is not None:
            first, second = first + up.astype(jnp.float32), second + down.astype(jnp.float32)
        first, second = first.astype(jnp.bfloat16), second.astype(jnp.bfloat16)
        if up is None and behind:
            first, second = lax.optimization_barrier((first, second) + behind)[:2]
        up = lax.ppermute(first, "expert", [(j, j + 1) for j in range(0, min(step, n - 1))])
        down = lax.ppermute(
            second, "expert", [(j, j - 1) for j in range(max(n - step, 1), n)]
        )
        if step == 1:
            mark = (up, down)
    return parts[0] + up.astype(jnp.float32) + down.astype(jnp.float32), mark


def coefficients(routes, gates, place):
    n = lax.axis_size("expert")
    result = []
    for r in range(n):
        target = lax.rem(place + r, n)
        value = jnp.sum(jnp.where(routes == target, gates, 0.0), axis=-1)
        if r:
            value = lax.ppermute(value, "expert", [(j, (j + r) % n) for j in range(n)])
        result.append(value)
    return result


def times(rows, weight):
    return jnp.dot(rows, weight, preferred_element_type=jnp.float32)


def times_transposed(rows, weight):
    return lax.dot_general(rows, weight, (((1,), (1,)), ((), ())), preferred_element_type=jnp.float32)


def on_device(
    fwd_tokens,
    fwd_routes,
    fwd_gates,
    bwd_saved,
    bwd_grads,
    bwd_routes,
    bwd_gates,
    w_up,
    w_down,
    query_latent,
    key_latent,
    query_weight,
    key_weight,
):
    n = lax.axis_size("expert")
    place = lax.axis_index("expert")
    core = lax.axis_index("dp")
    tok = fwd_tokens.shape[1]

    tokens_half = own_half(fwd_tokens[0], 1, core)
    saved_half = own_half(bwd_saved[0], 1, core)
    grads_half = own_half(bwd_grads[0], 1, core)
    routes = jnp.stack([fwd_routes[0], bwd_routes[0]])
    gates = jnp.stack([fwd_gates[0], bwd_gates[0]])
    latent = jnp.concatenate([query_latent[0, 0], key_latent[0, 0]], axis=1)

    tokens_all, mark, last = spread(tokens_half, place)
    up_own = own_half(w_up[0, 0], 0, core)
    up_other = swap(other_half(w_up[0, 0], 0, core))
    down_own = own_half(w_down[0, 0], 1, core)
    down_other = swap(other_half(w_down[0, 0], 1, core))
    coef = coefficients(routes, gates, place)
    saved_all, mark, last = spread(after(saved_half, *mark), place)
    grads_all, mark, last = spread(after(grads_half, *mark), place)
    latent_all, mark, last = spread(after(latent, *last), place)

    rows = jnp.concatenate(tokens_all, axis=0)
    pre_act = times(rows, up_own) + swap(times(rows, up_other))
    hidden = jax.nn.silu(pre_act).astype(jnp.bfloat16)
    out = times(hidden, down_own) + times(swap(hidden), down_other)
    parts = [out[r * tok:(r + 1) * tok] * coef[r][0][:, None] for r in range(n)]
    total, mark = collect(parts)
    section_half = (tokens_half.astype(jnp.float32) + total).astype(jnp.bfloat16)
    fwd_half = shifted(section_half, "pipe", 1)

    rows = jnp.concatenate(saved_all, axis=0)
    pre_act = times(rows, up_own) + swap(times(rows, up_other))
    rows = jnp.concatenate(grads_all, axis=0)
    back = times_transposed(rows, down_own) + swap(times_transposed(rows, down_other))
    pre_grad = (back * silu_grad(pre_act)).astype(jnp.bfloat16)
    pre_grad_other = swap(pre_grad)
    bwd_pieces, mark = [], ()
    width = grads_half.shape[1] // PIECES
    for k in range(PIECES):
        cut = slice(k * width, (k + 1) * width)
        out = times_transposed(pre_grad, up_own[cut]) + times_transposed(pre_grad_other, up_other[cut])
        parts = [out[r * tok:(r + 1) * tok] * coef[r][1][:, None] for r in range(n)]
        total, mark = collect(parts, mark)
        grad_piece = (grads_half[:, cut].astype(jnp.float32) + total).astype(jnp.bfloat16)
        bwd_pieces.append(shifted(grad_piece, "pipe", -1))

    query_proj = query_weight[0]
    key_proj = key_weight[0]
    heads_here = query_proj.shape[1] // HD
    latents = jnp.concatenate(latent_all, axis=0)
    seq_len = latents.shape[0]
    per = seq_len // n
    owners = lax.rem(place - jnp.arange(n, dtype=jnp.int32) + n, n)
    pos = (owners[:, None] * per + jnp.arange(per, dtype=jnp.int32)[None, :]).reshape(-1)
    rank = query_proj.shape[0]
    queries = times(latents[:, :rank], query_proj).astype(jnp.bfloat16).reshape(seq_len, heads_here, HD)
    keys = times(latents[:, rank:], key_proj).astype(jnp.bfloat16).reshape(seq_len, heads_here, HD)
    scores = jnp.einsum("qhd,khd->hqk", queries, keys, preferred_element_type=jnp.float32) * logit_scale
    scores = jnp.where((pos[:, None] >= pos[None, :])[None], scores, -1e30)
    local_max = jnp.max(scores, axis=(1, 2))
    head_max = jnp.maximum(local_max, swap(local_max))
    factor = jnp.sqrt(clip_limit / jnp.maximum(head_max, clip_limit))
    col_factor = jnp.repeat(factor, HD)
    query_clipped = (query_proj.astype(jnp.float32) * col_factor[None, :]).astype(jnp.bfloat16)
    key_clipped = (key_proj.astype(jnp.float32) * col_factor[None, :]).astype(jnp.bfloat16)

    def whole(pieces):
        theirs = [swap(piece) for piece in pieces]
        first = [jnp.where(core == 0, a, b) for a, b in zip(pieces, theirs)]
        second = [jnp.where(core == 0, b, a) for a, b in zip(pieces, theirs)]
        return jnp.concatenate(first + second, axis=1)

    return (whole([fwd_half])[None], whole(bwd_pieces)[None], query_clipped[None], key_clipped[None])


def solution(mesh):
    rows3 = P("pipe", "expert", None)
    in_specs = (rows3,) * 7 + (
        P("pipe", "expert", None, "dp"),
        P("pipe", "expert", "dp", None),
        P("pipe", "dp", "expert", None),
        P("pipe", "dp", "expert", None),
        P("pipe", None, "expert"),
        P("pipe", None, "expert"),
    )
    out_specs = (rows3, rows3, P("pipe", None, "expert"), P("pipe", None, "expert"))
    return jax.shard_map(
        on_device, mesh=mesh, in_specs=in_specs, out_specs=out_specs, check_vma=False
    )
```

```python
import jax
import jax.numpy as jnp
from jax import lax
from jax.sharding import PartitionSpec as P

HD = 128
PIECES = 1
LANES = 128

clip_limit = 100.0
logit_scale = 192.0 ** (-0.5)


def silu_grad(pre_act):
    sigmoid_val = jax.nn.sigmoid(pre_act)
    return sigmoid_val * (1.0 + pre_act * (1.0 - sigmoid_val))


def swap(block):
    return lax.ppermute(block, "dp", [(0, 1), (1, 0)])


def own_half(array, axis, core):
    width = array.shape[axis] // 2
    return lax.dynamic_slice_in_dim(array, core * width, width, axis)


def other_half(array, axis, core):
    width = array.shape[axis] // 2
    return lax.dynamic_slice_in_dim(array, (1 - core) * width, width, axis)


def after(block, *earlier):
    return lax.optimization_barrier((block,) + earlier)[0]


def shifted(block, axis, distance):
    devices = range(lax.axis_size(axis))
    route = [(i - distance, i) for i in devices if i - distance in devices]
    return lax.ppermute(block, axis, route)


def spread(block, place, beside=()):
    n = lax.axis_size("expert")
    up, down = [block], [block]
    for step in range(1, n):
        higher, lower = up[-1], down[-1]
        if step > 1:
            extra = tuple(beside) if step == 2 else ()
            higher, lower = lax.optimization_barrier((higher, lower) + extra)[:2]
        up.append(lax.ppermute(higher, "expert", [(j, j + 1) for j in range(step - 1, n - 1)]))
        down.append(lax.ppermute(lower, "expert", [(j, j - 1) for j in range(1, n - step + 1)]))
    blocks = [block] + [jnp.where(place >= r, up[r], down[n - r]) for r in range(1, n)]
    marks = [(up[min(s, n - 1)], down[min(s, n - 1)]) for s in (1, 2)]
    return blocks, marks


def collect(parts, behind=()):
    n = lax.axis_size("expert")
    up = down = None
    for step in range(1, n):
        first, second = parts[step], parts[n - step]
        if up is not None:
            first, second = first + up.astype(jnp.float32), second + down.astype(jnp.float32)
        first, second = first.astype(jnp.bfloat16), second.astype(jnp.bfloat16)
        extra = behind if up is None else ()
        first, second = lax.optimization_barrier((first, second) + extra)[:2]
        up = lax.ppermute(first, "expert", [(j, j + 1) for j in range(0, min(step, n - 1))])
        down = lax.ppermute(
            second, "expert", [(j, j - 1) for j in range(max(n - step, 1), n)]
        )
        if step == 1:
            mark = (up, down)
    return parts[0] + up.astype(jnp.float32) + down.astype(jnp.float32), mark


def gate_columns(routes, gates):
    experts = jnp.arange(LANES // 2, dtype=jnp.int32)
    hit = routes[:, :, None] == experts[None, None, :]
    return jnp.sum(jnp.where(hit, gates[:, :, None], 0.0), axis=1)


def column_of(block, index):
    lanes = jnp.arange(block.shape[1], dtype=jnp.int32)
    return jnp.sum(jnp.where(lanes[None, :] == index, block.astype(jnp.float32), 0.0), axis=1)


def times(rows, weight):
    return jnp.dot(rows, weight, preferred_element_type=jnp.float32)


def times_transposed(rows, weight):
    return lax.dot_general(rows, weight, (((1,), (1,)), ((), ())), preferred_element_type=jnp.float32)


def on_device(
    fwd_tokens,
    fwd_routes,
    fwd_gates,
    bwd_saved,
    bwd_grads,
    bwd_routes,
    bwd_gates,
    w_up,
    w_down,
    query_latent,
    key_latent,
    query_weight,
    key_weight,
):
    n = lax.axis_size("expert")
    place = lax.axis_index("expert")
    core = lax.axis_index("dp")
    tok = fwd_tokens.shape[1]

    tokens_half = own_half(fwd_tokens[0], 1, core)
    saved_half = own_half(bwd_saved[0], 1, core)
    grads_half = own_half(bwd_grads[0], 1, core)
    weighing = jnp.concatenate(
        [gate_columns(fwd_routes[0], fwd_gates[0]), gate_columns(bwd_routes[0], bwd_gates[0])], axis=1
    ).astype(jnp.bfloat16)
    latent = jnp.concatenate([query_latent[0, 0], key_latent[0, 0]], axis=1)

    width_half = tokens_half.shape[1]
    up_own = own_half(w_up[0, 0], 0, core)
    up_other = swap(other_half(w_up[0, 0], 0, core))
    down_own = own_half(w_down[0, 0], 1, core)
    down_other = swap(other_half(w_down[0, 0], 1, core))
    packed = jnp.concatenate([tokens_half, weighing], axis=1)
    packed_all, marks = spread(packed, place, (up_other, down_other))
    tokens_all = [block[:, :width_half] for block in packed_all]
    coef = [
        (column_of(block[:, width_half:], place), column_of(block[:, width_half:], place + LANES // 2))
        for block in packed_all
    ]
    saved_all, marks = spread(after(saved_half, *marks[1]), place)
    latent_all, marks = spread(after(latent, *marks[1]), place)
    grads_all, unused = spread(after(grads_half, *marks[1]), place, latent_all)

    rows = jnp.concatenate(tokens_all, axis=0)
    pre_act = times(rows, up_own) + swap(times(rows, up_other))
    hidden = jax.nn.silu(pre_act).astype(jnp.bfloat16)
    out = times(hidden, down_own) + times(swap(hidden), down_other)
    parts = [out[r * tok:(r + 1) * tok] * coef[r][0][:, None] for r in range(n)]
    total, mark = collect(parts)
    section_half = (tokens_half.astype(jnp.float32) + total).astype(jnp.bfloat16)
    fwd_half = shifted(section_half, "pipe", 1)

    rows = jnp.concatenate(saved_all, axis=0)
    pre_act = times(rows, up_own) + swap(times(rows, up_other))
    rows = jnp.concatenate(grads_all, axis=0)
    back = times_transposed(rows, down_own) + swap(times_transposed(rows, down_other))
    pre_grad = (back * silu_grad(pre_act)).astype(jnp.bfloat16)
    pre_grad_other = swap(pre_grad)
    bwd_pieces, mark = [], ()
    width = grads_half.shape[1] // PIECES
    for k in range(PIECES):
        cut = slice(k * width, (k + 1) * width)
        out = times_transposed(pre_grad, up_own[cut]) + times_transposed(pre_grad_other, up_other[cut])
        parts = [out[r * tok:(r + 1) * tok] * coef[r][1][:, None] for r in range(n)]
        total, mark = collect(parts, mark or (section_half,))
        grad_piece = (grads_half[:, cut].astype(jnp.float32) + total).astype(jnp.bfloat16)
        bwd_pieces.append(shifted(grad_piece, "pipe", -1))

    query_proj = query_weight[0]
    key_proj = key_weight[0]
    heads_here = query_proj.shape[1] // HD
    latents = jnp.concatenate(latent_all, axis=0)
    seq_len = latents.shape[0]
    per = seq_len // n
    owners = lax.rem(place - jnp.arange(n, dtype=jnp.int32) + n, n)
    pos = (owners[:, None] * per + jnp.arange(per, dtype=jnp.int32)[None, :]).reshape(-1)
    rank = query_proj.shape[0]
    queries = times(latents[:, :rank], query_proj).astype(jnp.bfloat16).reshape(seq_len, heads_here, HD)
    keys = times(latents[:, rank:], key_proj).astype(jnp.bfloat16).reshape(seq_len, heads_here, HD)
    scores = jnp.einsum("qhd,khd->hqk", queries, keys, preferred_element_type=jnp.float32) * logit_scale
    scores = jnp.where((pos[:, None] >= pos[None, :])[None], scores, -1e30)
    local_max = jnp.max(scores, axis=(1, 2))
    head_max = jnp.maximum(local_max, swap(local_max))
    factor = jnp.sqrt(clip_limit / jnp.maximum(head_max, clip_limit))
    col_factor = jnp.repeat(factor, HD)
    query_clipped = (query_proj.astype(jnp.float32) * col_factor[None, :]).astype(jnp.bfloat16)
    key_clipped = (key_proj.astype(jnp.float32) * col_factor[None, :]).astype(jnp.bfloat16)

    def whole(pieces):
        theirs = [swap(piece) for piece in pieces]
        first = [jnp.where(core == 0, a, b) for a, b in zip(pieces, theirs)]
        second = [jnp.where(core == 0, b, a) for a, b in zip(pieces, theirs)]
        return jnp.concatenate(first + second, axis=1)

    return (whole([fwd_half])[None], whole(bwd_pieces)[None], query_clipped[None], key_clipped[None])


def solution(mesh):
    rows3 = P("pipe", "expert", None)
    in_specs = (rows3,) * 7 + (
        P("pipe", "expert", None, "dp"),
        P("pipe", "expert", "dp", None),
        P("pipe", "dp", "expert", None),
        P("pipe", "dp", "expert", None),
        P("pipe", None, "expert"),
        P("pipe", None, "expert"),
    )
    out_specs = (rows3, rows3, P("pipe", None, "expert"), P("pipe", None, "expert"))
    return jax.shard_map(
        on_device, mesh=mesh, in_specs=in_specs, out_specs=out_specs, check_vma=False
    )
```
